256 devices in a mesh: row: 16 (over z_lo, x, core), col: 16 (over z_hi, y).
Axes of the slice: x: 4, y: 4, z: 8 (z_hi: 4, z_lo: 2; z = z_hi * 2 + z_lo), core: 2. Of those that a mesh axis runs over, the one named last changes fastest.
Arguments:
- hamiltonian: bfloat16 [4096, 4096], P('row', 'col'), may hold values from -9 to 9
- density: bfloat16 [4096, 4096], P('row', 'col'), may hold values from -9 to 9
- pattern: int32 [16, 16], P('row', 'col'), may hold values from 0 to 1, as said below
Outputs:
- gradient: float32 [4096, 4096], P('row', 'col')
- final_density: bfloat16 [4096, 4096], P('row', 'col')
The draws below stay inside these ranges and needn't reach their ends.
Inputs may be any that keep to these rules, and one draw needn't show every extreme that they name: pattern is symmetric and its diagonal is all ones.
All inputs are finite; a program needn't handle non-finite values.
Results may differ from the reference program's by a relative error of at most 0.0053.
Values may be sent and summed in bfloat16 or wider, within the bound.
No kernel may reach another device: no remote copies, remote signals or barrier semaphores. Data moves between devices by JAX's collectives and lax.ppermute only.
A program may use at most 64 MiB of HBM per device.

```python
import jax
import jax.numpy as jnp

B = 256
STEPS = 2
NB = 16


def draw_hamiltonian(key, part):
    key = jax.random.fold_in(key, 11)
    width = NB * B
    base = jax.random.normal(key, (width, width), jnp.float32)
    return jnp.clip((base + base.T) * 0.7071, -9.0, 9.0).astype(jnp.bfloat16)


def draw_density(key, part):
    key = jax.random.fold_in(key, 12)
    width = NB * B
    base = jax.random.normal(key, (width, width), jnp.float32)
    return jnp.clip((base + base.T) * 0.7071, -9.0, 9.0).astype(jnp.bfloat16)


def draw_pattern(key, part):
    key = jax.random.fold_in(key, 13)
    votes = jax.random.randint(key, (NB, NB), 0, 100)
    votes = jnp.minimum(votes, votes.T)
    places = jnp.arange(NB)
    spacing = jnp.abs(places[:, None] - places[None, :])
    spacing = jnp.minimum(spacing, NB - spacing)
    limit = 85 - 60 * spacing // max(NB // 2, 1)
    return jnp.where((spacing == 0) | (votes < limit), 1, 0).astype(jnp.int32)


def setup_inputs(seed: int = 0) -> dict:
    splits = jax.random.split(jax.random.key(seed), 4)
    return {
        "hamiltonian": draw_hamiltonian(jax.random.fold_in(splits[3], 71), 0),
        "density": draw_density(jax.random.fold_in(splits[3], 71), 0),
        "pattern": draw_pattern(jax.random.fold_in(splits[3], 71), 0),
    }


step_rate = 0.1

def apply_pattern(entries, pattern):
    blocks = pattern.shape[0]
    tile_size = entries.shape[0] // blocks
    shaped = entries.reshape(blocks, tile_size, blocks, tile_size) * pattern.astype(entries.dtype)[:, None, :, None]
    return shaped.reshape(entries.shape)

def reference(hamiltonian, density, pattern):
    ham_masked = apply_pattern(hamiltonian, pattern)
    dens_masked = apply_pattern(density, pattern)
    scaling = 1.0 / jnp.sqrt(jnp.float32(NB * B))
    gradient = jnp.zeros(hamiltonian.shape, jnp.float32)
    for iteration in range(STEPS):
        forward = jnp.dot(ham_masked, dens_masked, preferred_element_type=jnp.float32)
        product = apply_pattern(forward * scaling, pattern).astype(jnp.bfloat16)
        mirror = product.T
        triple = apply_pattern(jnp.dot(dens_masked, product, preferred_element_type=jnp.float32) * scaling, pattern)
        gradient = product.astype(jnp.float32) + mirror.astype(jnp.float32) - 2.0 * triple
        dens_masked = (dens_masked.astype(jnp.float32) - step_rate * gradient).astype(jnp.bfloat16)
    return (gradient, dens_masked)
```

```python
import itertools

import jax
import jax.numpy as jnp
from jax import lax
from jax.experimental import pallas as pl
from jax.experimental.pallas import tpu as pltpu
from jax.sharding import Mesh
from jax.sharding import PartitionSpec as P

STEPS = 2
RATE = 0.1
ROW = ("zlo", "x", "core")
COL = ("zhi", "y")
SIZES = {"zlo": 2, "x": 4, "core": 2, "zhi": 4, "y": 4}
VMEM = pl.BlockSpec(memory_space=pltpu.VMEM)
SMEM = pl.BlockSpec(memory_space=pltpu.SMEM)
F32, BF16 = jnp.float32, jnp.bfloat16


def fetch(value, **offsets):
    axes = tuple(offsets)
    sizes = [SIZES[a] for a in axes]
    pairs = []
    for place in itertools.product(*[range(n) for n in sizes]):
        source = dest = 0
        for here, size, a in zip(place, sizes, axes):
            source = source * size + (here + offsets[a]) % size
            dest = dest * size + here
        pairs.append((source, dest))
    return lax.ppermute(value, axes, pairs)


def transposed(value):
    return lax.ppermute(value, ROW + COL, [(16 * i + j, 16 * j + i) for i in range(16) for j in range(16)])


def gather_rows(block):
    near = [(1, 0), (0, 1), (0, 3), (1, 1), (1, 3), (0, 2), (1, 2)]
    same = {(0, 0): block}
    for z, x in near:
        same[z, x] = fetch(block, zlo=z, x=x)
    arrays, offsets = [], []
    for group in ([(0, 0)], near[:4], near[4:]):
        held = jnp.concatenate([same[g][None] for g in group], 0)
        for core, array in ((0, held), (1, fetch(held, core=1))):
            arrays.append(array)
            offsets.append([(z, x, core) for z, x in group])
    return arrays, offsets


def gather_cols(block):
    one = block[None]
    around = jnp.concatenate([fetch(one, zhi=1), fetch(one, zhi=3)], 0)
    far = fetch(one, zhi=2)
    arrays, offsets = [], []
    for held, zs in ((one, [0]), (around, [1, 3]), (far, [2])):
        for y in (0, 1, 3, 2):
            arrays.append(held if y == 0 else fetch(held, y=y))
            offsets.append([(z, y) for z in zs])
    return arrays, offsets


def assemble_kernel(counts, place_ref, *refs):
    out_ref = refs[-1]
    at = 0
    for ref, count in zip(refs[:-1], counts):
        for part in range(count):
            out_ref[place_ref[at]] = ref[part]
            at += 1


def assemble(arrays, place):
    counts = [a.shape[0] for a in arrays]
    return pl.pallas_call(
        lambda *refs: assemble_kernel(counts, *refs),
        out_shape=jax.ShapeDtypeStruct((16, 256, 256), BF16),
        in_specs=[SMEM] + [VMEM] * len(arrays),
        out_specs=VMEM,
        name="assemble",
    )(place, *arrays)


def total(place_ref, panel_ref, refs, counts):
    acc = jnp.zeros((256, 256), F32)
    at = 0
    for ref, count in zip(refs, counts):
        for part in range(count):
            acc += jnp.dot(panel_ref[place_ref[at]], ref[part], preferred_element_type=F32)
            at += 1
    return acc


def product_kernel(counts, keep_ref, place_ref, panel_ref, *refs):
    acc = total(place_ref, panel_ref, refs[:-1], counts)
    refs[-1][...] = (acc * (keep_ref[0, 0].astype(F32) / 64.0)).astype(BF16)


def product_of(keep, place, panel, arrays):
    counts = [a.shape[0] for a in arrays]
    return pl.pallas_call(
        lambda *refs: product_kernel(counts, *refs),
        out_shape=jax.ShapeDtypeStruct((256, 256), BF16),
        in_specs=[SMEM, SMEM] + [VMEM] * (1 + len(arrays)),
        out_specs=VMEM,
        name="product",
    )(keep, place, panel, *arrays)


def update_kernel(counts, last, keep_ref, place_ref, panel_ref, dens_ref, prod_ref, turned_ref, *refs):
    n = len(counts)
    acc = total(place_ref, panel_ref, refs[:n], counts)
    triple = acc * (keep_ref[0, 0].astype(F32) / 64.0)
    mirror = turned_ref[...].T.astype(F32)
    gradient = prod_ref[...].astype(F32) + mirror - 2.0 * triple
    refs[n][...] = (dens_ref[...].astype(F32) - RATE * gradient).astype(BF16)
    if last:
        refs[n + 1][...] = gradient


def update_of(last, keep, place, panel, dens, prod, turned, arrays):
    counts = [a.shape[0] for a in arrays]
    outs = [jax.ShapeDtypeStruct((256, 256), BF16)]
    if last:
        outs.append(jax.ShapeDtypeStruct((256, 256), F32))
    return pl.pallas_call(
        lambda *refs: update_kernel(counts, last, *refs),
        out_shape=outs,
        in_specs=[SMEM, SMEM] + [VMEM] * (4 + len(arrays)),
        out_specs=[VMEM] * len(outs),
        name="update",
    )(keep, place, panel, dens, prod, turned, *arrays)


def row_places(offsets):
    zlo, x, core = (lax.axis_index(a) for a in ROW)
    flat = [o for group in offsets for o in group]
    return jnp.stack([((zlo + a) % 2) * 8 + ((x + b) % 4) * 2 + (core + c) % 2 for a, b, c in flat]).astype(jnp.int32)


def col_places(offsets):
    zhi, y = (lax.axis_index(a) for a in COL)
    flat = [o for group in offsets for o in group]
    return jnp.stack([((zhi + a) % 4) * 4 + (y + b) % 4 for a, b in flat]).astype(jnp.int32)


def local(hamiltonian, density, pattern):
    keep = pattern.astype(BF16)
    ham = hamiltonian * keep
    dens = density * keep
    parts, offsets = gather_cols(ham)
    col_at = col_places(offsets)
    ham_panel = assemble(parts, col_at)
    for step in range(STEPS):
        cols, offsets = gather_rows(dens)
        row_at = row_places(offsets)
        parts, _ = gather_cols(dens)
        product = product_of(pattern, row_at, ham_panel, cols)
        prod_cols, _ = gather_rows(product)
        turned = transposed(product)
        dens_panel = assemble(parts, col_at)
        outs = update_of(step == STEPS - 1, pattern, row_at, dens_panel, dens, product, turned, prod_cols)
        dens = outs[0]
    return outs[1], dens


def solution(mesh):
    fine = Mesh(mesh.devices.reshape(2, 4, 2, 4, 4), ROW + COL)
    return jax.shard_map(
        local,
        mesh=fine,
        in_specs=(P(ROW, COL), P(ROW, COL), P(ROW, COL)),
        out_specs=(P(ROW, COL), P(ROW, COL)),
        check_vma=False,
    )
```

```python
import itertools

import jax
import jax.numpy as jnp
from jax import lax
from jax.experimental import pallas as pl
from jax.experimental.pallas import tpu as pltpu
from jax.sharding import Mesh
from jax.sharding import PartitionSpec as P

STEPS = 2
RATE = 0.1
ROW = ("zlo", "x", "core")
COL = ("zhi", "y")
SIZES = {"zlo": 2, "x": 4, "core": 2, "zhi": 4, "y": 4}
FIRST = ((0, 2, 3, 1), (2, 0, 1, 3))
VMEM = pl.BlockSpec(memory_space=pltpu.VMEM)
SMEM = pl.BlockSpec(memory_space=pltpu.SMEM)
F32, BF16 = jnp.float32, jnp.bfloat16
BLOCK = jax.ShapeDtypeStruct((256, 256), BF16)
BLOCK32 = jax.ShapeDtypeStruct((256, 256), F32)


def fetch(value, **offsets):
    axes = tuple(offsets)
    sizes = [SIZES[a] for a in axes]
    pairs = []
    for place in itertools.product(*[range(n) for n in sizes]):
        source = dest = 0
        for here, size, a in zip(place, sizes, axes):
            source = source * size + (here + offsets[a]) % size
            dest = dest * size + here
        pairs.append((source, dest))
    return lax.ppermute(value, axes, pairs)


def transposed(value):
    return lax.ppermute(value, ROW + COL, [(16 * i + j, 16 * j + i) for i in range(16) for j in range(16)])


def after(value, *others):
    return lax.optimization_barrier((value, *others))[0]


def call(kernel, outs, args, name, megabytes=4, flops=0):
    moved = sum(a.size * a.dtype.itemsize for a in args) + sum(o.size * o.dtype.itemsize for o in outs)
    return pl.pallas_call(
        kernel,
        out_shape=outs,
        in_specs=[SMEM if a.dtype == jnp.int32 else VMEM for a in args],
        out_specs=[VMEM] * len(outs),
        compiler_params=pltpu.CompilerParams(vmem_limit_bytes=megabytes << 20),
        cost_estimate=pl.CostEstimate(flops=flops, bytes_accessed=moved, transcendentals=0),
        name=name,
    )(*args)


def mask_kernel(keep_ref, ham_ref, dens_ref, ham_out, dens_out):
    keep = keep_ref[0, 0].astype(F32)
    ham_out[...] = (ham_ref[...].astype(F32) * keep).astype(BF16)
    dens_out[...] = (dens_ref[...].astype(F32) * keep).astype(BF16)


def pack_kernel(*refs):
    for n, ref in enumerate(refs[:-1]):
        refs[-1][n] = ref[...]


def pack(blocks):
    return call(pack_kernel, [jax.ShapeDtypeStruct((len(blocks), 256, 256), BF16)], blocks, "pack")[0]


def multiply_kernel(at_ref, *refs):
    panel, (held_ref, swapped_ref, mine_ref, other_ref) = refs[:-4], refs[-4:]
    acc = jnp.zeros((512, 256), F32)
    for n, ref in enumerate(panel):
        place = at_ref[2 * n]
        block = jnp.where(at_ref[2 * n + 1] == 0, held_ref[place], swapped_ref[place])
        acc += jnp.dot(ref[...].reshape(512, 256), block, preferred_element_type=F32)
    acc = acc * (1.0 / 64.0)
    first, second = acc[:256], acc[256:]
    mine_first = at_ref[16] == 0
    mine_ref[...] = jnp.where(mine_first, first, second)
    other_ref[...] = jnp.where(mine_first, second, first).astype(BF16)


def multiply(at, panel, columns):
    return call(multiply_kernel, [BLOCK32, BLOCK], [at, *panel, *columns], "multiply", 12, 2 * 4096 * 256 * 256)


def product_kernel(keep_ref, mine_ref, other_ref, out_ref):
    out_ref[...] = ((mine_ref[...] + other_ref[...].astype(F32)) * keep_ref[0, 0].astype(F32)).astype(BF16)


def update_kernel(keep_ref, mine_ref, other_ref, prod_ref, turned_ref, dens_ref, *outs):
    triple = (mine_ref[...] + other_ref[...].astype(F32)) * keep_ref[0, 0].astype(F32)
    gradient = prod_ref[...].astype(F32) + turned_ref[...].T.astype(F32) - 2.0 * triple
    outs[0][...] = (dens_ref[...].astype(F32) - RATE * gradient).astype(BF16)
    if len(outs) == 2:
        outs[1][...] = gradient


PANEL = ((0, 0), (0, 1), (1, 0), (1, 1), (3, 0), (3, 1), (2, 0), (2, 1))
AROUND = (0, 1, 3, 2)


def start_z(block, ms):
    pieces = []
    for m in ms:
        pairs = []
        for zlo in range(2):
            for zhi in range(4):
                source = 4 * zlo + (FIRST[zlo][zhi] ^ m)
                pairs.append(((source % 2) * 4 + source // 2, zlo * 4 + zhi))
        pieces.append(lax.ppermute(block, ("zlo", "zhi"), pairs))
    return pieces


def gather_panel(block):
    z = start_z(block, range(4))
    a, b = pack(z[:2]), pack(z[2:])
    up_a, down_a = fetch(a, y=1), fetch(a, y=3)
    up_b, down_b = fetch(b, y=1), fetch(b, y=3)
    return [a, b, up_a, up_b, down_a, down_b, fetch(up_a, y=1), fetch(down_b, y=3)]


def gather_x(block):
    held = pack([block, fetch(block, x=1), fetch(block, x=3), fetch(block, x=2)])
    return [held, fetch(held, core=1)]


def places():
    zlo, x, core, zhi, y = (lax.axis_index(a) for a in ROW + COL)
    first = jnp.take(jnp.array(FIRST, jnp.int32).reshape(-1), zlo * 4 + zhi)
    rows = []
    for dy, pair in PANEL:
        column = (y + dy) % 4
        dx = ((pair ^ (first // 2)) * 2 + column // 2 - x) % 4
        rows += [jnp.where(dx == 0, 0, jnp.where(dx == 1, 1, jnp.where(dx == 3, 2, 3))), (column % 2) ^ core]
    rows.append((first % 2) ^ zlo)
    return jnp.stack(rows).astype(jnp.int32)


def local(hamiltonian, density, pattern):
    at = places()
    ham, dens = call(mask_kernel, [BLOCK, BLOCK], [pattern, hamiltonian, density], "mask")
    ham_panel = gather_panel(ham)
    for step in range(STEPS):
        last = step == STEPS - 1
        dens_cols = gather_x(dens)
        dens_panel = gather_panel(dens)
        mine, other = multiply(at, ham_panel, dens_cols)
        product = call(product_kernel, [BLOCK], [pattern, mine, fetch(other, zlo=1)], "product")[0]
        prod_cols = gather_x(product)
        turned = transposed(product)
        mine, other = multiply(at, dens_panel, prod_cols)
        outs = call(
            update_kernel,
            [BLOCK, BLOCK32] if last else [BLOCK],
            [pattern, mine, fetch(other, zlo=1), product, turned, dens],
            "update",
        )
        dens = outs[0]
    return outs[1], dens


def solution(mesh):
    fine = Mesh(mesh.devices.reshape(2, 4, 2, 4, 4), ROW + COL)
    return jax.shard_map(
        local,
        mesh=fine,
        in_specs=(P(ROW, COL), P(ROW, COL), P(ROW, COL)),
        out_specs=(P(ROW, COL), P(ROW, COL)),
        check_vma=False,
    )
```

```python
import itertools

import jax
import jax.numpy as jnp
from jax import lax
from jax.experimental import pallas as pl
from jax.experimental.pallas import tpu as pltpu
from jax.sharding import Mesh
from jax.sharding import PartitionSpec as P

STEPS = 2
RATE = 0.1
ROW = ("zlo", "x", "core")
COL = ("zhi", "y")
SIZES = {"zlo": 2, "x": 4, "core": 2, "zhi": 4, "y": 4}
VMEM = pl.BlockSpec(memory_space=pltpu.VMEM)
SMEM = pl.BlockSpec(memory_space=pltpu.SMEM)
F32, BF16 = jnp.float32, jnp.bfloat16
BLOCK = jax.ShapeDtypeStruct((256, 256), BF16)
PAIR = jax.ShapeDtypeStruct((2, 256, 256), BF16)
BLOCK32 = jax.ShapeDtypeStruct((256, 256), F32)


def fetch(value, **offsets):
    axes = tuple(offsets)
    sizes = [SIZES[a] for a in axes]
    pairs = []
    for place in itertools.product(*[range(n) for n in sizes]):
        source = dest = 0
        for here, size, a in zip(place, sizes, axes):
            source = source * size + (here + offsets[a]) % size
            dest = dest * size + here
        pairs.append((source, dest))
    return lax.ppermute(value, axes, pairs)


def transposed(value):
    return lax.ppermute(value, ROW + COL, [(16 * i + j, 16 * j + i) for i in range(16) for j in range(16)])


def after(value, *others):
    return lax.optimization_barrier((value, *others))[0]


def call(kernel, outs, args, name, megabytes=4, flops=0):
    moved = sum(a.size * a.dtype.itemsize for a in args) + sum(o.size * o.dtype.itemsize for o in outs)
    return pl.pallas_call(
        kernel,
        out_shape=outs,
        in_specs=[SMEM if a.dtype == jnp.int32 else VMEM for a in args],
        out_specs=[VMEM] * len(outs),
        compiler_params=pltpu.CompilerParams(vmem_limit_bytes=megabytes << 20),
        cost_estimate=pl.CostEstimate(flops=flops, bytes_accessed=moved, transcendentals=0),
        name=name,
    )(*args)


def mask_kernel(keep_ref, in_ref, out_ref):
    out_ref[...] = (in_ref[...].astype(F32) * keep_ref[0, 0].astype(F32)).astype(BF16)


def pack_kernel(*refs):
    for n, ref in enumerate(refs[:-1]):
        refs[-1][n] = ref[...]


def pack(blocks):
    return call(pack_kernel, [jax.ShapeDtypeStruct((len(blocks), 256, 256), BF16)], blocks, "pack")[0]


def split_kernel(up_ref, down_ref, low_ref, high_ref):
    low_ref[...] = up_ref[:2]
    high_ref[...] = down_ref[2:]


def total(at_ref, refs):
    panel, (held_ref, swapped_ref) = refs[:-2], refs[-2:]
    acc = jnp.zeros((256, 256), F32)
    n = 0
    for ref in panel:
        for part in range(ref.shape[0]):
            place = at_ref[2 * n]
            block = jnp.where(at_ref[2 * n + 1] == 0, held_ref[place], swapped_ref[place])
            acc += jnp.dot(ref[part], block, preferred_element_type=F32)
            n += 1
    return acc


def product_kernel(keep_ref, at_ref, *refs):
    acc = total(at_ref, refs[:-1])
    refs[-1][...] = (acc * (keep_ref[0, 0].astype(F32) / 64.0)).astype(BF16)


def update_kernel(keep_ref, at_ref, prod_ref, turned_ref, dens_ref, *refs):
    refs, outs = refs[:7], refs[7:]
    triple = total(at_ref, refs) * (keep_ref[0, 0].astype(F32) / 64.0)
    gradient = prod_ref[...].astype(F32) + turned_ref[...].T.astype(F32) - 2.0 * triple
    outs[0][...] = (dens_ref[...].astype(F32) - RATE * gradient).astype(BF16)
    if len(outs) == 2:
        outs[1][...] = gradient


PANEL = ((0, (0, 1, 3, 2)), (1, (0, 1, 3, 2)), (3, (0, 1, 3, 2)), (2, (0, 1)), (2, (3, 2)))
FLOPS = 2 * 4096 * 256 * 256


def gather_z(block):
    return [block, fetch(block, zhi=1), fetch(block, zhi=3), fetch(block, zhi=2)]


def gather_y(held, *others):
    up, down = fetch(held, y=1), fetch(held, y=3)
    low, high = call(split_kernel, [PAIR, PAIR], [up, down], "split")
    return [held, up, down, fetch(after(low, *others), y=1), fetch(after(high, *others), y=3)]


def gather_x(block, early=(), late=()):
    pair = pack([block, fetch(block, zlo=1)])
    sent = after(pair, *early)
    held = join([pair, fetch(sent, x=1), fetch(sent, x=3), fetch(sent, x=2)])
    return [held, fetch(after(held, *late), core=1)]


def join_kernel(*refs):
    for n, ref in enumerate(refs[:-1]):
        refs[-1][2 * n : 2 * n + 2] = ref[...]


def join(pairs):
    return call(join_kernel, [jax.ShapeDtypeStruct((2 * len(pairs), 256, 256), BF16)], pairs, "join")[0]


def places():
    zlo, x, core, zhi, y = (lax.axis_index(a) for a in ROW + COL)
    rows = []
    for dy, dz in ((dy, dz) for dy, offsets in PANEL for dz in offsets):
        k = (zhi + dz) % 4 * 4 + (y + dy) % 4
        dx = (k // 2 % 4 - x) % 4
        step = jnp.where(dx == 0, 0, jnp.where(dx == 1, 1, jnp.where(dx == 3, 2, 3)))
        rows += [step * 2 + (k // 8 ^ zlo), (k % 2) ^ core]
    return jnp.stack(rows).astype(jnp.int32)


def local(hamiltonian, density, pattern):
    at = places()
    ham = call(mask_kernel, [BLOCK], [pattern, hamiltonian], "mask")[0]
    dens = call(mask_kernel, [BLOCK], [pattern, density], "mask")[0]
    ham_z = pack(gather_z(ham))
    ham_panel = gather_y(ham_z)
    dens = after(dens, ham_z)
    for step in range(STEPS):
        last = step == STEPS - 1
        dens_z = pack(gather_z(dens))
        dens_cols = gather_x(dens, (), (dens_z,) if step else (dens_z, *ham_panel[3:]))
        product = call(product_kernel, [BLOCK], [pattern, at, *ham_panel, *dens_cols], "product", 12, FLOPS)[0]
        turned = transposed(product)
        dens_panel = gather_y(dens_z, turned)
        prod_cols = gather_x(product, (), dens_panel[3:])
        outs = call(
            update_kernel,
            [BLOCK, BLOCK32] if last else [BLOCK],
            [pattern, at, product, turned, dens, *dens_panel, *prod_cols],
            "update",
            12,
            FLOPS,
        )
        dens = outs[0]
    return outs[1], dens


def solution(mesh):
    fine = Mesh(mesh.devices.reshape(2, 4, 2, 4, 4), ROW + COL)
    return jax.shard_map(
        local,
        mesh=fine,
        in_specs=(P(ROW, COL), P(ROW, COL), P(ROW, COL)),
        out_specs=(P(ROW, COL), P(ROW, COL)),
        check_vma=False,
    )
```

```python
import itertools

import jax
import jax.numpy as jnp
from jax import lax
from jax.experimental import pallas as pl
from jax.experimental.pallas import tpu as pltpu
from jax.sharding import Mesh
from jax.sharding import PartitionSpec as P

STEPS = 2
RATE = 0.1
ROW = ("zlo", "x", "core")
COL = ("zhi", "y")
SIZES = {"zlo": 2, "x": 4, "core": 2, "zhi": 4, "y": 4}
VMEM = pl.BlockSpec(memory_space=pltpu.VMEM)
SMEM = pl.BlockSpec(memory_space=pltpu.SMEM)
F32, BF16 = jnp.float32, jnp.bfloat16
BLOCK = jax.ShapeDtypeStruct((256, 256), BF16)
PAIR = jax.ShapeDtypeStruct((2, 256, 256), BF16)
BLOCK32 = jax.ShapeDtypeStruct((256, 256), F32)


def fetch(value, **offsets):
    axes = tuple(offsets)
    sizes = [SIZES[a] for a in axes]
    pairs = []
    for place in itertools.product(*[range(n) for n in sizes]):
        source = dest = 0
        for here, size, a in zip(place, sizes, axes):
            source = source * size + (here + offsets[a]) % size
            dest = dest * size + here
        pairs.append((source, dest))
    return lax.ppermute(value, axes, pairs)


def transposed(value):
    return lax.ppermute(value, ROW + COL, [(16 * i + j, 16 * j + i) for i in range(16) for j in range(16)])


def after(value, *others):
    return lax.optimization_barrier((value, *others))[0]


def call(kernel, outs, args, name, megabytes=4, flops=0):
    moved = sum(a.size * a.dtype.itemsize for a in args) + sum(o.size * o.dtype.itemsize for o in outs)
    return pl.pallas_call(
        kernel,
        out_shape=outs,
        in_specs=[SMEM if a.dtype == jnp.int32 else VMEM for a in args],
        out_specs=[VMEM] * len(outs),
        compiler_params=pltpu.CompilerParams(vmem_limit_bytes=megabytes << 20),
        cost_estimate=pl.CostEstimate(flops=flops, bytes_accessed=moved, transcendentals=0),
        name=name,
    )(*args)


def mask_kernel(keep_ref, in_ref, out_ref):
    out_ref[...] = (in_ref[...].astype(F32) * keep_ref[0, 0].astype(F32)).astype(BF16)


def pack_kernel(*refs):
    for n, ref in enumerate(refs[:-1]):
        refs[-1][n] = ref[...]


def pack(blocks):
    return call(pack_kernel, [jax.ShapeDtypeStruct((len(blocks), 256, 256), BF16)], blocks, "pack")[0]


def split_kernel(up_ref, down_ref, low_ref, high_ref):
    low_ref[...] = up_ref[:2]
    high_ref[...] = down_ref[2:]


def total(at_ref, refs):
    panel, (held_ref, swapped_ref) = refs[:-2], refs[-2:]
    acc = jnp.zeros((256, 256), F32)
    n = 0
    for ref in panel:
        for part in range(ref.shape[0]):
            place = at_ref[2 * n]
            block = jnp.where(at_ref[2 * n + 1] == 0, held_ref[place], swapped_ref[place])
            acc += jnp.dot(ref[part], block, preferred_element_type=F32)
            n += 1
    return acc


def product_kernel(keep_ref, at_ref, *refs):
    acc = total(at_ref, refs[:-1])
    refs[-1][...] = (acc * (keep_ref[0, 0].astype(F32) / 64.0)).astype(BF16)


def update_kernel(keep_ref, at_ref, prod_ref, turned_ref, dens_ref, *refs):
    refs, outs = refs[:7], refs[7:]
    triple = total(at_ref, refs) * (keep_ref[0, 0].astype(F32) / 64.0)
    gradient = prod_ref[...].astype(F32) + turned_ref[...].T.astype(F32) - 2.0 * triple
    outs[0][...] = (dens_ref[...].astype(F32) - RATE * gradient).astype(BF16)
    if len(outs) == 2:
        outs[1][...] = gradient


PANEL = ((0, (0, 1, 3, 2)), (1, (0, 1, 3, 2)), (3, (0, 1, 3, 2)), (2, (0, 1)), (2, (3, 2)))
FLOPS = 2 * 4096 * 256 * 256


def gather_z(block):
    return [block, fetch(block, zhi=1), fetch(block, zhi=3), fetch(block, zhi=2)]


def gather_y(held, *others):
    up, down = fetch(held, y=1), fetch(held, y=3)
    low, high = call(split_kernel, [PAIR, PAIR], [up, down], "split")
    return [held, up, down, fetch(after(low, *others), y=1), fetch(after(high, *others), y=3)]


def gather_x(block, early=(), late=()):
    pair = pack([block, fetch(block, zlo=1)])
    sent = after(pair, *early)
    held = join([pair, fetch(sent, x=1), fetch(sent, x=3), fetch(sent, x=2)])
    return [held, fetch(after(held, *late), core=1)]


def join_kernel(*refs):
    for n, ref in enumerate(refs[:-1]):
        refs[-1][2 * n : 2 * n + 2] = ref[...]


def join(pairs):
    return call(join_kernel, [jax.ShapeDtypeStruct((2 * len(pairs), 256, 256), BF16)], pairs, "join")[0]


def places_kernel(out_ref):
    zlo, x, core, zhi, y = (lax.axis_index(a) for a in ROW + COL)
    n = 0
    for dy, dz in ((dy, dz) for dy, offsets in PANEL for dz in offsets):
        k = ((zhi + dz) & 3) * 4 + ((y + dy) & 3)
        dx = ((k >> 1) - x) & 3
        out_ref[n] = (dx ^ (dx >> 1)) * 2 + ((k >> 3) ^ zlo)
        out_ref[n + 1] = (k & 1) ^ core
        n += 2


def places():
    return pl.pallas_call(
        places_kernel,
        out_shape=jax.ShapeDtypeStruct((32,), jnp.int32),
        out_specs=SMEM,
        compiler_params=pltpu.CompilerParams(vmem_limit_bytes=1 << 20),
        name="places",
    )()


def local(hamiltonian, density, pattern):
    at = places()
    ham = call(mask_kernel, [BLOCK], [pattern, hamiltonian], "mask")[0]
    dens = call(mask_kernel, [BLOCK], [pattern, density], "mask")[0]
    around = gather_z(ham)
    ham_z = pack([after(around[0], at), *around[1:]])
    ham_panel = gather_y(ham_z)
    for step in range(STEPS):
        last = step == STEPS - 1
        dens_z = pack(gather_z(dens if step else after(dens, ham_z)))
        dens_cols = gather_x(dens, () if step else (ham_z,), (dens_z,) if step else (dens_z, *ham_panel[3:]))
        product = call(product_kernel, [BLOCK], [pattern, at, *ham_panel, *dens_cols], "product", 12, FLOPS)[0]
        turned = transposed(product)
        dens_panel = gather_y(dens_z, turned)
        prod_cols = gather_x(product, (), dens_panel[3:])
        outs = call(
            update_kernel,
            [BLOCK, BLOCK32] if last else [BLOCK],
            [pattern, at, product, turned, dens, *dens_panel, *prod_cols],
            "update",
            12,
            FLOPS,
        )
        dens = outs[0]
    return outs[1], dens


def solution(mesh):
    fine = Mesh(mesh.devices.reshape(2, 4, 2, 4, 4), ROW + COL)
    return jax.shard_map(
        local,
        mesh=fine,
        in_specs=(P(ROW, COL), P(ROW, COL), P(ROW, COL)),
        out_specs=(P(ROW, COL), P(ROW, COL)),
        check_vma=False,
    )
```
